256 devices in a mesh: section: 8 (over z_hi, core), expert: 32 (over x, z_lo, y).
Axes of the slice: x: 4, y: 4, z: 8 (z_hi: 4, z_lo: 2; z = z_hi * 2 + z_lo), core: 2. Of those that a mesh axis runs over, the one named last changes fastest.
Arguments:
- arriving_state: bfloat16 [8, 4096, 4096], P('section', 'expert'), may hold values from -40 to 40
- stream_extent: int32 [8, 32], P('section', 'expert'), may hold values from 64 to 128, as said below
- word_specialist_choice: int32 [8, 4096], P('section', 'expert'), may hold values from 0 to 3
- capacity_places: int32 [8, 4096], P('section', 'expert'), may hold values from -1 to 39, as said below
- rescale_factors: float32 [8, 2, 4096], P('section'), may hold values from 0.1 to 1.9
- gating_columns: float32 [8, 4096, 4], P('section'), may hold values from -0.09375 to 0.09375
- specialist_entry_matrix: bfloat16 [8, 4096, 20480], P('section', None, 'expert'), may hold values from -0.09375 to 0.09375
- specialist_exit_matrix: bfloat16 [8, 20480, 4096], P('section', 'expert'), may hold values from -0.078125 to 0.078125
Outputs:
- section_out: bfloat16 [8, 4096, 4096], P('section', 'expert')
The draws below stay inside these ranges and needn't reach their ends.
Inputs may be any that keep to these rules, and one draw needn't show every extreme that they name: `stream_extent`: every section has one sequence of length 128 and one of length 64. `capacity_places`: for a token below its sequence's length: its rank among the earlier such tokens of the same device with the same expert, if that rank is under 40; else -1. Tokens at or beyond the length have -1. In every section one expert receives 40 tokens from every device.
All inputs are finite; a program needn't handle non-finite values.
Results may differ from the reference program's by a relative error of at most 0.008.
Values may be sent and summed in bfloat16 or wider, within the bound.
No kernel may reach another device: no remote copies, remote signals or barrier semaphores. Data moves between devices by JAX's collectives and lax.ppermute only.
A program may use at most 128 MiB of HBM per device.

```python
import jax
import jax.numpy as jnp
from jax import lax

D = 4096
HEAD_DIM = 64
HEADS = 64
FF = 5120
GROUP = 8
HID_DEV = 640
EXPERTS = 4
TOK_DEV = 128
CAP = 40
TOKENS = 4096
N_SECTION = 8
N_EXPERT = 32


def routing(key):
    base = jax.random.fold_in(key, 101)
    keys_all = jax.random.split(base, 6)
    lengths = jax.random.randint(keys_all[0], (N_SECTION, N_EXPERT), TOK_DEV // 2, TOK_DEV + 1)
    longest = jax.random.randint(keys_all[1], (N_SECTION,), 0, N_EXPERT)
    shortest = (longest + 1 + jax.random.randint(keys_all[2], (N_SECTION,), 0, N_EXPERT - 1)) % N_EXPERT
    column_ids = jnp.arange(N_EXPERT)
    lengths = jnp.where(column_ids[None, :] == longest[:, None], TOK_DEV, lengths)
    lengths = jnp.where(column_ids[None, :] == shortest[:, None], TOK_DEV // 2, lengths)
    hot_expert = jax.random.randint(keys_all[3], (N_SECTION,), 0, EXPERTS)
    raw_pick = jax.random.randint(keys_all[4], (N_SECTION, N_EXPERT, TOK_DEV), 0, 2 * EXPERTS)
    expert_pick = jnp.where(raw_pick < EXPERTS, raw_pick, hot_expert[:, None, None])
    positions = jnp.arange(TOK_DEV)
    priority = jax.random.randint(keys_all[5], (N_SECTION, N_EXPERT, TOK_DEV), 0, 2 ** 20) * TOK_DEV + positions
    priority = jnp.where(positions < TOK_DEV // 2, priority, 2 ** 30)
    order_pos = jnp.argsort(priority, axis=-1, stable=True)
    rank_pos = jnp.argsort(order_pos, axis=-1, stable=True)
    forced = rank_pos < CAP
    expert_pick = jnp.where(forced, hot_expert[:, None, None], expert_pick)
    is_live = positions[None, None, :] < lengths[:, :, None]
    onehot = ((expert_pick[..., None] == jnp.arange(EXPERTS)) & is_live[..., None]).astype(jnp.int32)
    running_count = jnp.cumsum(onehot, axis=2) - 1
    slot_raw = jnp.take_along_axis(running_count, expert_pick[..., None], axis=3)[..., 0]
    slot_ids = jnp.where(is_live & (slot_raw < CAP), slot_raw, -1)
    return (lengths.astype(jnp.int32), expert_pick.reshape(N_SECTION, TOKENS).astype(jnp.int32), slot_ids.reshape(N_SECTION, TOKENS).astype(jnp.int32))


def draw_stream_extent(key, part):
    return routing(key)[0]


def draw_word_specialist_choice(key, part):
    return routing(key)[1]


def draw_capacity_places(key, part):
    return routing(key)[2]


def draw_arriving_state(key, part):
    key = jax.random.fold_in(key, 7)
    noise_keys = jax.random.split(key, 1)
    dims = (N_SECTION, TOKENS, D)
    values = jnp.clip(jax.random.normal(noise_keys[0], dims, jnp.float32), -6.0, 6.0)
    return values.astype(jnp.bfloat16)


def block_scale(own_key, shape, cuts, smallest, high):
    level, own = 1.0, jax.random.fold_in(own_key, 6)
    for position, blocks in cuts:
        steps = jnp.exp(jax.random.uniform(jax.random.fold_in(own, position), (blocks,), jnp.float32, smallest / len(cuts), high / len(cuts)))
        level = level * jnp.repeat(steps, shape[position] // blocks).reshape([-1 if axis == position else 1 for axis in range(len(shape))])
    return level


def noise(key, shape, width, reach, pieces=(), kind=jnp.bfloat16):
    entries = width * jax.random.normal(key, shape, jnp.float32)
    if pieces:
        entries = entries * block_scale(key, shape, pieces, -0.22, 0.18)
    return jnp.clip(entries, -reach, reach).astype(kind)


def setup_inputs(seed: int = 0) -> dict:
    key_list = jax.random.split(jax.random.key(seed), 9)
    arriving_state = draw_arriving_state(jax.random.fold_in(key_list[8], 71), 0)
    stream_extent = draw_stream_extent(jax.random.fold_in(key_list[8], 71), 0)
    word_specialist_choice = draw_word_specialist_choice(jax.random.fold_in(key_list[8], 71), 0)
    capacity_places = draw_capacity_places(jax.random.fold_in(key_list[8], 71), 0)
    rescale_factors = jnp.clip(1.0 + 0.18 * jax.random.normal(key_list[4], (N_SECTION, 2, D), jnp.float32), 0.1, 1.9)
    gating_columns = noise(key_list[5], (N_SECTION, D, EXPERTS), D ** -0.5, 0.09375, ((0, 8),), jnp.float32)
    specialist_entry_matrix = noise(key_list[6], (N_SECTION, D, EXPERTS * FF), D ** -0.5, 0.09375, ((0, 8), (2, 32)))
    specialist_exit_matrix = noise(key_list[7], (N_SECTION, EXPERTS * FF, D), FF ** -0.5, 0.078125, ((0, 8), (1, 32)))
    return dict(arriving_state=arriving_state, stream_extent=stream_extent, word_specialist_choice=word_specialist_choice, capacity_places=capacity_places, rescale_factors=rescale_factors, gating_columns=gating_columns, specialist_entry_matrix=specialist_entry_matrix, specialist_exit_matrix=specialist_exit_matrix)


def rms_scale(values, gain_row):
    mean_sq = lax.optimization_barrier(jnp.mean(values * values, axis=-1, keepdims=True))
    return values * lax.rsqrt(mean_sq + 1e-06) * gain_row

def expert_section(buffers, w_first, w_second):

    def per_expert(expert_index):
        in_rows = buffers[expert_index]
        running = jnp.zeros((in_rows.shape[0], D), jnp.float32)
        for part_index in range(GROUP):
            column_start = ((expert_index * GROUP + part_index) * HID_DEV).astype(jnp.int32)
            first_part = lax.dynamic_slice_in_dim(w_first, column_start, HID_DEV, 1)
            second_part = lax.dynamic_slice_in_dim(w_second, column_start, HID_DEV, 0)
            hidden = jnp.maximum(jnp.dot(in_rows, first_part, preferred_element_type=jnp.float32), 0.0).astype(jnp.bfloat16)
            partial_out = jnp.dot(hidden, second_part, preferred_element_type=jnp.float32).astype(jnp.bfloat16)
            running = running + partial_out.astype(jnp.float32)
        return running
    return lax.map(per_expert, jnp.arange(EXPERTS, dtype=jnp.int32))

def reference(arriving_state, stream_extent, word_specialist_choice, capacity_places, rescale_factors, gating_columns, specialist_entry_matrix, specialist_exit_matrix):
    enc_count = N_SECTION // 2
    slot_total = EXPERTS * N_EXPERT * CAP
    layer_outs = []
    for segment_ordinal in range(N_SECTION):
        latent_activation = arriving_state[segment_ordinal].astype(jnp.float32)
        normed = rms_scale(latent_activation, rescale_factors[segment_ordinal, 0]).astype(jnp.bfloat16)
        logits = jnp.dot(normed.astype(jnp.float32), gating_columns[segment_ordinal], precision=lax.Precision.HIGHEST)
        chosen = word_specialist_choice[segment_ordinal]
        slot_ids = capacity_places[segment_ordinal]
        is_live = slot_ids >= 0
        gate_value = jax.nn.sigmoid(jnp.take_along_axis(logits, chosen[:, None], axis=1)[:, 0])
        source = (jnp.arange(TOKENS, dtype=jnp.int32) // TOK_DEV).astype(jnp.int32)
        target = ((chosen * N_EXPERT + source) * CAP + jnp.maximum(slot_ids, 0)).astype(jnp.int32)
        where_to = jnp.where(is_live, target, slot_total).astype(jnp.int32)
        buffers = jnp.zeros((slot_total, D), jnp.bfloat16).at[where_to].set(normed, mode='drop')
        buffers = buffers.reshape(EXPERTS, N_EXPERT * CAP, D)
        results = expert_section(buffers, specialist_entry_matrix[segment_ordinal], specialist_exit_matrix[segment_ordinal]).reshape(slot_total, D)
        picked = results[jnp.where(is_live, target, 0).astype(jnp.int32)]
        mixed_sum = latent_activation + jnp.where(is_live, gate_value, 0.0)[:, None] * picked
        layer_outs.append(mixed_sum.astype(jnp.bfloat16))
    memory = rms_scale(layer_outs[enc_count - 1].astype(jnp.float32), rescale_factors[enc_count - 1, 1]).astype(jnp.bfloat16)
    key_rows = memory.astype(jnp.float32).reshape(N_EXPERT, TOK_DEV, HEADS, HEAD_DIM)
    source_len = stream_extent[enc_count - 1]
    key_live = jnp.arange(TOK_DEV, dtype=jnp.int32)[None, :] < source_len[:, None]
    for segment_ordinal in range(enc_count, N_SECTION):
        layer_now = layer_outs[segment_ordinal].astype(jnp.float32)
        queries = rms_scale(layer_now, rescale_factors[segment_ordinal, 1]).astype(jnp.bfloat16)
        queries = queries.astype(jnp.float32).reshape(N_EXPERT, TOK_DEV, HEADS, HEAD_DIM)
        scores = jnp.einsum('pqhd,pkhd->phqk', queries, key_rows, precision=lax.Precision.HIGHEST) / jnp.sqrt(jnp.float32(HEAD_DIM))
        scores = jnp.where(key_live[:, None, None, :], scores, jnp.float32(-1e+30))
        row_top = lax.optimization_barrier(jnp.max(scores, axis=-1, keepdims=True))
        expo = jnp.exp(scores - row_top)
        weights = (expo / lax.optimization_barrier(jnp.sum(expo, axis=-1, keepdims=True))).astype(jnp.bfloat16)
        context = jnp.einsum('phqk,pkhd->pqhd', weights.astype(jnp.float32), key_rows, precision=lax.Precision.HIGHEST)
        context = context.reshape(TOKENS, D)
        layer_outs[segment_ordinal] = (layer_now + context).astype(jnp.bfloat16)
    return jnp.stack(layer_outs)
```

```python
import jax
import jax.numpy as jnp
from jax import lax
from jax.sharding import PartitionSpec as P

HEAD_DIM = 64
CAP = 40
NX, NZ, NY = 4, 2, 4
CHUNKS = ((0, 1152, 2048), (2048, 3200, 4096))
PLACE = (0, 40, 120, 80)


def shift(value, dx=0, dz=0, dy=0):
    pairs = []
    for x in range(NX):
        for z in range(NZ):
            for y in range(NY):
                to = ((x + dx) % NX * NZ + (z + dz) % NZ) * NY + (y + dy) % NY
                pairs.append(((x * NZ + z) * NY + y, to))
    return lax.ppermute(value, "expert", pairs)


def dot32(a, b):
    return jnp.dot(a, b, preferred_element_type=jnp.float32)


def half(value):
    return value.astype(jnp.bfloat16)


def rms_scale(values, gain_row):
    mean_sq = jnp.mean(values * values, axis=-1, keepdims=True)
    return values * lax.rsqrt(mean_sq + 1e-06) * gain_row


def after(value, *earlier):
    return lax.optimization_barrier((value, *earlier))[0]


def rows(*blocks):
    return jnp.concatenate(blocks, axis=0)


def gather(packed, w_first):
    def first(*blocks):
        h = half(jnp.maximum(dot32(rows(*blocks), w_first), 0.0))
        cuts, start = [], 0
        for block in blocks:
            cuts.append(h[start : start + block.shape[0]])
            start += block.shape[0]
        return cuts

    p0, p1, p3, p2 = packed[:40], packed[40:80], packed[80:120], packed[120:]
    r2 = shift(p2, dx=2)
    r1 = shift(p1, dx=1)
    r3 = shift(p3, dx=-1)
    b0 = shift(p0, dy=1)
    a0 = shift(p0, dy=-1)
    fb0 = shift(after(b0[:24], a0), dy=1)
    fa0 = shift(after(a0[24:], b0), dy=-1)
    o0 = shift(after(p0, r1, r3), dz=1)
    g1 = rows(r1, r3, r2)
    b1 = shift(g1, dy=1)
    a1 = shift(g1, dy=-1)
    po = shift(after(g1[:88], fb0, fa0), dz=1)
    rest0 = rows(b0, a0, fb0, fa0)
    or0 = shift(after(rest0, o0), dz=1)
    h_p0, h_b0, h_a0, h_fb0, h_fa0 = first(p0, b0, a0, fb0, fa0)
    pb = shift(after(po, b1, a1), dy=1)
    pa = shift(after(po, b1, a1), dy=-1)
    h_g1, h_b1, h_a1 = first(g1, b1, a1)
    fb1 = shift(after(b1[:64], po, h_b1), dy=1)
    fa1 = shift(after(a1[64:], po, h_b1), dy=-1)
    zq = shift(after(rows(g1[88:], b1[88:], a1[88:]), or0), dz=1)
    h_o0, h_or0 = first(o0, or0)
    pbh = shift(after(pb[:48], pa), dy=1)
    pah = shift(after(pa[48:], pb), dy=-1)
    h_po, h_pb, h_pa = first(po, pb, pa)
    zqf = shift(after(fa1[24:], fb1), dz=1)
    h_fb1, h_fa1 = first(fb1, fa1)
    (h_zq,) = first(zq)
    h_pbh, h_pah, h_zqf = first(pbh, pah, zqf)
    return {
        (0, 0): rows(h_p0, h_g1),
        (0, -1): rows(h_b0, h_b1),
        (0, 1): rows(h_a0, h_a1),
        (0, 2): rows(h_fb0, h_fa0, h_fb1, h_fa1),
        (1, 0): rows(h_o0, h_po, h_zq[:32]),
        (1, -1): rows(h_or0[:40], h_pb, h_zq[32:64]),
        (1, 1): rows(h_or0[40:80], h_pa, h_zq[64:]),
        (1, 2): rows(h_or0[80:], h_pbh, h_pah, h_zqf),
    }


def reduce_chunks(hid, w_second, chunks):
    f32 = jnp.float32
    a = {k: v[:80] for k, v in hid.items()}
    b = {k: v[80:] for k, v in hid.items()}
    up1 = rows(a[1, 2], a[0, 2], b[1, 1], b[0, 1])
    down1 = rows(b[1, 2], b[0, 2], a[1, -1], a[0, -1])
    up2 = rows(a[1, 1], a[0, 1])
    down2 = rows(b[1, -1], b[0, -1])
    own_a = rows(a[1, 0], a[0, 0])
    own_b = rows(b[1, 0], b[0, 0])
    away = rows(hid[1, 2], hid[1, 1], hid[1, -1], hid[1, 0])
    up3 = rows(a[0, 2], b[0, 1])
    down3 = rows(b[0, 2], a[0, -1])
    totals = []
    gate_y, gate_z = (), ()
    for y_cols, z_cols in chunks:
        wy, wz = w_second[:, y_cols], w_second[:, z_cols]
        g = shift(after(half(dot32(away, wz)), *gate_z), dz=1)
        ru = shift(after(half(dot32(up1, wy)), *gate_y), dy=1)
        rd = shift(after(half(dot32(down1, wy)), *gate_y), dy=-1)
        su = shift(half(dot32(up2, wy) + ru[:160].astype(f32)), dy=1)
        sd = shift(half(dot32(down2, wy) + rd[:160].astype(f32)), dy=-1)
        g2, g1, gm, g0 = g[:160], g[160:320], g[320:480], g[480:]
        tu = shift(half(dot32(up3, wz) + rows(g2[:80], g1[80:]).astype(f32)), dy=1)
        td = shift(half(dot32(down3, wz) + rows(g2[80:], gm[:80]).astype(f32)), dy=-1)
        sum_a = dot32(own_a, wy) + rd[160:].astype(f32) + su.astype(f32)
        sum_b = dot32(own_b, wy) + ru[160:].astype(f32) + sd.astype(f32)
        e = shift(half(rows(sum_a[:80], sum_b[:80])), dz=1)
        vu = shift(half(dot32(a[0, 1], wz) + g1[:80].astype(f32) + tu[:80].astype(f32)), dy=1)
        vd = shift(half(dot32(b[0, -1], wz) + gm[80:].astype(f32) + td[:80].astype(f32)), dy=-1)
        total_y = half(rows(sum_a[80:], sum_b[80:]) + e.astype(f32))
        total_a = dot32(a[0, 0], wz) + g0[:80].astype(f32) + td[80:].astype(f32) + vu.astype(f32)
        total_b = dot32(b[0, 0], wz) + g0[80:].astype(f32) + tu[80:].astype(f32) + vd.astype(f32)
        total_z = half(rows(total_a, total_b))
        totals.append(jnp.concatenate([total_y, total_z], axis=1))
        gate_y, gate_z = (su, sd), (e,)
    return totals


def body(
    arriving_state,
    stream_extent,
    word_specialist_choice,
    capacity_places,
    rescale_factors,
    gating_columns,
    specialist_entry_matrix,
    specialist_exit_matrix,
):
    f32 = jnp.float32
    acts = arriving_state[0]
    row_count, features = acts.shape
    enc_count = lax.axis_size("section") // 2
    section_index = lax.axis_index("section")
    my_x = lax.axis_index("expert") // (NZ * NY)
    gain_rows = rescale_factors[0]
    route_cols = gating_columns[0]
    experts = route_cols.shape[1]
    w_first = specialist_entry_matrix[0]
    w_second = specialist_exit_matrix[0]

    acts_wide = acts.astype(f32)
    normed = rms_scale(acts_wide, gain_rows[0]).astype(jnp.bfloat16)
    chosen = word_specialist_choice[0]
    slot_ids = capacity_places[0]
    is_live = slot_ids >= 0
    ahead = (chosen - my_x + NX) % NX
    start = jnp.where(ahead == 2, PLACE[2], jnp.where(ahead == 3, PLACE[3], ahead * CAP))
    target = jnp.where(is_live, start + slot_ids, -1)
    places = jnp.arange(experts * CAP, dtype=jnp.int32)
    dispatch_map = (places[:, None] == target[None, :]).astype(jnp.bfloat16)
    packed = half(dot32(dispatch_map, normed))

    hid = gather(packed, w_first)

    logits = jnp.dot(normed.astype(f32), route_cols, precision=lax.Precision.HIGHEST)
    picks = chosen[:, None] == jnp.arange(experts, dtype=jnp.int32)[None, :]
    gate_value = jax.nn.sigmoid(jnp.sum(jnp.where(picks, logits, 0.0), axis=1))
    gate = jnp.where(is_live, gate_value, 0.0)[:, None]
    combine_map = (target[:, None] == places[None, :]).astype(jnp.bfloat16)

    gain = gain_rows[1]
    high = half(gain)
    mid = half(gain - high.astype(f32))
    low = half(gain - high.astype(f32) - mid.astype(f32))
    length = jnp.full((features,), stream_extent[0, 0].astype(jnp.bfloat16))
    extra = jnp.concatenate([jnp.stack([high, mid, low, length]), jnp.zeros((4, features), jnp.bfloat16)])
    odd = section_index % 2 == 1

    layer_cols, source_cols, extra_cols = [], [], []
    n = row_count // 2
    chunks = [(slice(a, b), slice(b, c)) for a, b, c in CHUNKS]
    for (lo, _, hi), total in zip(CHUNKS, reduce_chunks(hid, w_second, chunks)):
        back = rows(
            total[:40],
            shift(total[40:80], dx=-1),
            shift(total[80:120], dx=1),
            shift(total[120:160], dx=-2),
        )
        cols = half(acts_wide[:, lo:hi] + gate * dot32(combine_map, back))
        layer_cols.append(cols)
        parts = [rows(cols[:n], extra[:, lo:hi]), rows(cols[n:], extra[:, lo:hi])]
        mine = sum(
            lax.ppermute(parts[s % 2], "section", [(enc_count - 1, s)])
            for s in range(enc_count, 2 * enc_count)
        )
        other = lax.ppermute(mine, "section", [(s, s ^ 1) for s in range(enc_count, 2 * enc_count)])
        source_cols.append(
            rows(jnp.where(odd, other[:n], mine[:n]), jnp.where(odd, mine[:n], other[:n]))
        )
        extra_cols.append(mine[n:])
    extra = jnp.concatenate(extra_cols, axis=1).astype(f32)
    memory_gain = extra[0] + extra[1] + extra[2]
    source_len = extra[3, 0].astype(jnp.int32)
    layer_out = jnp.concatenate(layer_cols, axis=1)
    source = jnp.concatenate(source_cols, axis=1)
    side_rows = rms_scale(layer_out.astype(f32), gain_rows[1]).astype(jnp.bfloat16)
    memory = rms_scale(source.astype(f32), memory_gain).astype(jnp.bfloat16)

    head_count = features // HEAD_DIM
    queries = side_rows.reshape(row_count, head_count, HEAD_DIM)
    key_rows = memory.reshape(row_count, head_count, HEAD_DIM)
    scores = jnp.einsum("qhd,khd->hqk", queries, key_rows, preferred_element_type=f32)
    scores = scores / jnp.sqrt(f32(HEAD_DIM))
    key_live = jnp.arange(row_count, dtype=jnp.int32) < source_len
    scores = jnp.where(key_live[None, None, :], scores, f32(-1e30))
    row_top = jnp.max(scores, axis=-1, keepdims=True)
    expo = jnp.exp(scores - row_top)
    weights = (expo / jnp.sum(expo, axis=-1, keepdims=True)).astype(jnp.bfloat16)
    context = jnp.einsum("hqk,khd->qhd", weights, key_rows, preferred_element_type=f32)
    decoded = (layer_out.astype(f32) + context.reshape(row_count, features)).astype(jnp.bfloat16)
    return jnp.where(section_index >= enc_count, decoded, layer_out)[None]


def solution(mesh):
    placed = (
        P("section", "expert", None),
        P("section", "expert"),
        P("section", "expert"),
        P("section", "expert"),
        P("section", None, None),
        P("section", None, None),
        P("section", None, "expert"),
        P("section", "expert", None),
    )
    return jax.shard_map(
        body, mesh=mesh, in_specs=placed, out_specs=P("section", "expert", None), check_vma=False
    )
```

```python
import jax
import jax.numpy as jnp
from jax import lax
from jax.experimental import pallas as pl
from jax.experimental.pallas import tpu as pltpu
from jax.sharding import PartitionSpec as P

HEAD_DIM = 64
CAP = 40
NX, NZ, NY = 4, 2, 4
CHUNKS = ((0, 1152, 2048), (2048, 3200, 4096))
PLACE = (0, 40, 120, 80)


def shift(value, dx=0, dz=0, dy=0):
    pairs = []
    for x in range(NX):
        for z in range(NZ):
            for y in range(NY):
                to = ((x + dx) % NX * NZ + (z + dz) % NZ) * NY + (y + dy) % NY
                pairs.append(((x * NZ + z) * NY + y, to))
    return lax.ppermute(value, "expert", pairs)


def dot32(a, b):
    return jnp.dot(a, b, preferred_element_type=jnp.float32)


def half(value):
    return value.astype(jnp.bfloat16)


def rms_scale(values, gain_row):
    mean_sq = jnp.mean(values * values, axis=-1, keepdims=True)
    return values * lax.rsqrt(mean_sq + 1e-06) * gain_row


def after(value, *earlier):
    return lax.optimization_barrier((value, *earlier))[0]


def rows(*blocks):
    return jnp.concatenate(blocks, axis=0)


def gather(p0, p1, p3, p2, w_first):
    def first(*blocks):
        h = half(jnp.maximum(dot32(rows(*blocks), w_first), 0.0))
        cuts, start = [], 0
        for block in blocks:
            cuts.append(h[start : start + block.shape[0]])
            start += block.shape[0]
        return cuts

    r2 = shift(p2, dx=2)
    r1 = shift(p1, dx=1)
    r3 = shift(p3, dx=-1)
    b0 = shift(p0, dy=1)
    a0 = shift(p0, dy=-1)
    o0 = shift(after(p0, b0, a0), dz=1)
    g1 = after(rows(r1, r3, r2), o0)
    b1 = shift(g1, dy=1)
    a1 = shift(g1, dy=-1)
    po = shift(g1[:88], dz=1)
    h_p0, h_b0, h_a0 = first(p0, b0, a0)
    near0 = shift(after(rows(b0, a0), po), dz=1)
    fb = shift(after(rows(b0[:16], b1[:64]), a1), dy=1)
    fa = shift(after(rows(a0[16:], a1[64:]), b1), dy=-1)
    h_g1, h_b1, h_a1 = first(after(g1, near0), b1, a1)
    zq = shift(after(rows(g1[88:], b1[88:], a1[88:]), near0), dz=1)
    pb = shift(after(po, near0), dy=1)
    pa = shift(after(po, near0), dy=-1)
    h_o0, h_near0 = first(o0, near0)
    h_fb, h_fa = first(fb, fa)
    zf = shift(after(rows(fb[:16], fa[:24], fa[48:]), zq), dz=1)
    pbh = shift(after(pb[:48], pa), dy=1)
    pah = shift(after(pa[48:], pb), dy=-1)
    h_po, h_pb, h_pa = first(po, pb, pa)
    (h_zq,) = first(zq)
    h_pbh, h_pah, h_zf = first(pbh, pah, zf)
    return {
        (0, 0): rows(h_p0, h_g1),
        (0, -1): rows(h_b0, h_b1),
        (0, 1): rows(h_a0, h_a1),
        (0, 2): rows(h_fb[:16], h_fa[:24], h_fb[16:], h_fa[24:]),
        (1, 0): rows(h_o0, h_po, h_zq[:32]),
        (1, -1): rows(h_near0[:40], h_pb, h_zq[32:64]),
        (1, 1): rows(h_near0[40:], h_pa, h_zq[64:]),
        (1, 2): rows(h_zf[:40], h_pbh, h_pah, h_zf[40:]),
    }


def reduce_chunks(hid, w_second, chunks):
    f32 = jnp.float32
    a = {k: v[:80] for k, v in hid.items()}
    b = {k: v[80:] for k, v in hid.items()}
    up1 = rows(a[1, 2], a[0, 2], b[1, 1], b[0, 1])
    down1 = rows(b[1, 2], b[0, 2], a[1, -1], a[0, -1])
    up2 = rows(a[1, 1], a[0, 1])
    down2 = rows(b[1, -1], b[0, -1])
    up3 = rows(a[0, 2], b[0, 1])
    down3 = rows(b[0, 2], a[0, -1])
    own_a = rows(a[1, 0], a[0, 0])
    own_b = rows(b[1, 0], b[0, 0])
    away = rows(hid[1, 2], hid[1, 1], hid[1, -1], hid[1, 0])
    (wy1, wz1), (wy2, wz2) = [(w_second[:, y], w_second[:, z]) for y, z in chunks]

    def part(h, w, *more):
        out = dot32(h, w)
        for m in more:
            out = out + m.astype(f32)
        return half(out)

    def start(w, *earlier):
        ru = shift(after(part(up1, w), *earlier), dy=1)
        rd = shift(after(part(down1, w), *earlier), dy=-1)
        return ru, rd

    def second(w, ru, rd, *earlier):
        su = shift(after(part(up2, w, ru[:160]), *earlier), dy=1)
        sd = shift(after(part(down2, w, rd[:160]), *earlier), dy=-1)
        return su, sd

    def sums(w, ru, rd, su, sd):
        sum_a = dot32(own_a, w) + rd[160:].astype(f32) + su.astype(f32)
        sum_b = dot32(own_b, w) + ru[160:].astype(f32) + sd.astype(f32)
        return half(rows(sum_a[:80], sum_b[:80])), rows(sum_a[80:], sum_b[80:])

    def third(w, g, *earlier):
        tu = shift(after(part(up3, w, rows(g[:80], g[240:320])), *earlier), dy=1)
        td = shift(after(part(down3, w, rows(g[80:160], g[320:400])), *earlier), dy=-1)
        return tu, td

    def fourth(w, g, tu, td):
        vu = shift(part(a[0, 1], w, g[160:240], tu[:80]), dy=1)
        vd = shift(part(b[0, -1], w, g[400:480], td[:80]), dy=-1)
        return vu, vd

    def total(w, g, kept, e, tu, td, vu, vd):
        z = rows(
            part(a[0, 0], w, g[480:560], td[80:], vu), part(b[0, 0], w, g[560:], tu[80:], vd)
        )
        return jnp.concatenate([half(kept + e.astype(f32)), z], axis=1)

    ru1, rd1 = start(wy1)
    g1 = shift(part(away, wz1), dz=1)
    su1, sd1 = second(wy1, ru1, rd1)
    ru2, rd2 = start(wy2, ru1, rd1)
    g2 = shift(after(part(away, wz2), g1), dz=1)
    tu1, td1 = third(wz1, g1, su1, sd1)
    su2, sd2 = second(wy2, ru2, rd2)
    sent1, kept1 = sums(wy1, ru1, rd1, su1, sd1)
    vu1, vd1 = fourth(wz1, g1, tu1, td1)
    e1 = shift(after(sent1, g2), dz=1)
    tu2, td2 = third(wz2, g2, su2, sd2)
    sent2, kept2 = sums(wy2, ru2, rd2, su2, sd2)
    e2 = shift(after(sent2, vu1, vd1, e1), dz=1)
    vu2, vd2 = fourth(wz2, g2, tu2, td2)
    total1 = total(wz1, g1, kept1, e1, tu1, td1, vu1, vd1)
    total2 = total(wz2, g2, kept2, e2, tu2, td2, vu2, vd2)
    return total1, total2


def full(memory_space=pltpu.VMEM):
    return pl.BlockSpec(memory_space=memory_space)


def dispatch_kernel(x_ref, acts_ref, gain_ref, chosen_ref, slot_ref, *outs):
    f32 = jnp.float32
    count, features = acts_ref.shape
    step = 512
    square = jnp.zeros((count, 128), f32)
    for c in range(0, features, step):
        v = acts_ref[:, c : c + step].astype(f32)
        v = v * v
        for k in range(0, step, 128):
            square = square + v[:, k : k + 128]
    scale = lax.rsqrt(jnp.sum(square, axis=1, keepdims=True) / features + 1e-06)
    ahead = (chosen_ref[...] - x_ref[0] + NX) & (NX - 1)
    slot = slot_ref[...]
    maps = []
    for d in (0, 1, 3, 2):
        place = jnp.where((slot >= 0) & (ahead == d), slot, -1)
        maps.append((lax.broadcasted_iota(jnp.int32, (CAP, count), 0) == place).astype(jnp.bfloat16))
    for c in range(0, features, step):
        cols = slice(c, c + step)
        normed = (acts_ref[:, cols].astype(f32) * scale * gain_ref[0:1, cols]).astype(jnp.bfloat16)
        for out, pick in zip(outs, maps):
            out[:, cols] = dot32(pick, normed).astype(jnp.bfloat16)


def dispatch(my_x, acts, gains, chosen, slots):
    features = acts.shape[1]
    block = jax.ShapeDtypeStruct((CAP, features), jnp.bfloat16)
    return pl.pallas_call(
        dispatch_kernel,
        out_shape=[block] * 4,
        in_specs=[full(pltpu.SMEM)] + [full()] * 4,
        out_specs=[full()] * 4,
        compiler_params=pltpu.CompilerParams(vmem_limit_bytes=24 << 20),
        cost_estimate=pl.CostEstimate(flops=4 * 160 * 128 * features, bytes_accessed=4 << 20, transcendentals=128),
    )(my_x.reshape(1), acts, gains, chosen, slots)


def attention_kernel(decoder_ref, lay1, lay2, n1, f1, b1, n2, f2, b2, gain_ref, out_ref, side, memory):
    f32 = jnp.float32
    count, first = lay1.shape
    features = out_ref.shape[1]
    decoder = decoder_ref[0]
    step = 256

    def lay_cols(c):
        return lay1[:, c : c + step] if c < first else lay2[:, c - first : c - first + step]

    def source_cols(c, part):
        refs, c = ((n1, f1, b1), c) if c < first else ((n2, f2, b2), c - first)
        near, far, beside = [ref[part, c : c + step].astype(f32) for ref in refs]
        return near + far + beside

    @pl.when(decoder == 0)
    def _():
        for c in range(0, features, step):
            out_ref[:, c : c + step] = lay_cols(c)

    @pl.when(decoder == 1)
    def _():
        squares = [jnp.zeros((count, 128), f32), jnp.zeros((count, 128), f32)]
        token_rows, extra_rows = slice(0, count), slice(count, count + 16)
        for c in range(0, features, step):
            source = source_cols(c, token_rows)
            memory[:, c : c + step] = source.astype(jnp.bfloat16)
            for i, v in enumerate((lay_cols(c).astype(f32), source)):
                v = v * v
                for k in range(0, step, 128):
                    squares[i] = squares[i] + v[:, k : k + 128]
        scales = [lax.rsqrt(jnp.sum(s, axis=1, keepdims=True) / features + 1e-06) for s in squares]
        for c in range(0, features, step):
            cols = slice(c, c + step)
            side[:, cols] = (lay_cols(c).astype(f32) * scales[0] * gain_ref[1:2, cols]).astype(jnp.bfloat16)
            extra = source_cols(c % first + first, extra_rows)[4 * (c // first) :]
            gain = extra[0:1] + extra[1:2] + extra[2:3]
            memory[:, cols] = (memory[:, cols].astype(f32) * scales[1] * gain).astype(jnp.bfloat16)
        length = source_cols(first, extra_rows)[3:4, :count]
        live = lax.broadcasted_iota(jnp.int32, (1, count), 1).astype(f32) < length
        head_of = lax.broadcasted_iota(jnp.int32, (1, step), 1) // HEAD_DIM
        heads = step // HEAD_DIM
        for c in range(0, features, step):
            cols = slice(c, c + step)
            query, keys = side[:, cols], memory[:, cols]
            zero = jnp.zeros_like(query)
            stacked = rows(*[jnp.where(head_of == h, query, zero) for h in range(heads)])
            scores = lax.dot_general(
                stacked, keys, (((1,), (1,)), ((), ())), preferred_element_type=f32
            )
            scores = jnp.where(live, scores * (HEAD_DIM**-0.5), f32(-1e30))
            expo = jnp.exp(scores - jnp.max(scores, axis=1, keepdims=True))
            weights = (expo / jnp.sum(expo, axis=1, keepdims=True)).astype(jnp.bfloat16)
            found = dot32(weights, keys)
            context = jnp.zeros((count, step), f32)
            for h in range(heads):
                context = jnp.where(head_of == h, found[h * count : (h + 1) * count], context)
            out_ref[:, cols] = (lay_cols(c).astype(f32) + context).astype(jnp.bfloat16)


def attention(decoder, lay1, lay2, n1, f1, b1, n2, f2, b2, gains):
    count, features = lay1.shape[0], gains.shape[1]
    whole = (count, features)
    return pl.pallas_call(
        attention_kernel,
        out_shape=jax.ShapeDtypeStruct(whole, jnp.bfloat16),
        in_specs=[full(pltpu.SMEM)] + [full()] * 9,
        out_specs=full(),
        scratch_shapes=[pltpu.VMEM(whole, jnp.bfloat16)] * 2,
        compiler_params=pltpu.CompilerParams(vmem_limit_bytes=32 << 20),
        cost_estimate=pl.CostEstimate(flops=1 << 30, bytes_accessed=8 << 20, transcendentals=1 << 20),
    )(decoder.reshape(1), lay1, lay2, n1, f1, b1, n2, f2, b2, gains)


def body(
    arriving_state,
    stream_extent,
    word_specialist_choice,
    capacity_places,
    rescale_factors,
    gating_columns,
    specialist_entry_matrix,
    specialist_exit_matrix,
):
    f32 = jnp.float32
    acts = arriving_state[0]
    row_count, features = acts.shape
    enc_count = lax.axis_size("section") // 2
    section_index = lax.axis_index("section")
    my_x = lax.axis_index("expert") // (NZ * NY)
    gain_rows = rescale_factors[0]
    route_cols = gating_columns[0]
    experts = route_cols.shape[1]
    w_first = specialist_entry_matrix[0]
    w_second = specialist_exit_matrix[0]

    acts_wide = acts.astype(f32)
    normed = rms_scale(acts_wide, gain_rows[0]).astype(jnp.bfloat16)
    chosen = word_specialist_choice[0]
    slot_ids = capacity_places[0]
    is_live = slot_ids >= 0
    ahead = (chosen - my_x + NX) % NX
    start = jnp.where(ahead == 2, PLACE[2], jnp.where(ahead == 3, PLACE[3], ahead * CAP))
    target = jnp.where(is_live, start + slot_ids, -1)
    places = jnp.arange(experts * CAP, dtype=jnp.int32)
    blocks = dispatch(my_x, acts, gain_rows, word_specialist_choice, capacity_places)

    hid = gather(*blocks, w_first)

    logits = jnp.dot(normed.astype(f32), route_cols, precision=lax.Precision.HIGHEST)
    picks = chosen[:, None] == jnp.arange(experts, dtype=jnp.int32)[None, :]
    gate_value = jax.nn.sigmoid(jnp.sum(jnp.where(picks, logits, 0.0), axis=1))
    gate = jnp.where(is_live, gate_value, 0.0)[:, None]
    combine_map = (target[:, None] == places[None, :]).astype(jnp.bfloat16)

    gain = gain_rows[1]
    high = half(gain)
    mid = half(gain - high.astype(f32))
    low = half(gain - high.astype(f32) - mid.astype(f32))
    extra = jnp.stack([high, mid, low, jnp.full((features,), stream_extent[0, 0].astype(jnp.bfloat16))])
    extra = rows(extra[:, : features // 2], extra[:, features // 2 :], jnp.zeros((8, features // 2), jnp.bfloat16))
    layer_cols, source_cols = [], []
    chunks = [(slice(a, b), slice(b, c)) for a, b, c in CHUNKS]
    last = enc_count - 1
    for (lo, _, hi), total in zip(CHUNKS, reduce_chunks(hid, w_second, chunks)):
        kept = total[:40]
        if layer_cols:
            total = after(total, layer_cols[0])
            kept = after(kept, source_cols[0])
        back = rows(
            kept,
            shift(total[40:80], dx=-1),
            shift(total[80:120], dx=1),
            shift(total[120:160], dx=-2),
        )
        cols = half(acts_wide[:, lo:hi] + gate * dot32(combine_map, back))
        layer_cols.append(cols)
        message = cols if lo == 0 else rows(cols, extra)
        near = lax.ppermute(message, "section", [(last, last + 2)])
        far = lax.ppermute(near, "section", [(last + 2, last + 4)])
        beside = lax.ppermute(near + far, "section", [(last + 2, last + 1), (last + 4, last + 3)])
        source_cols += [near, far, beside]
    decoder = (section_index >= enc_count).astype(jnp.int32)
    return attention(decoder, *layer_cols, *source_cols, gain_rows)[None]


def solution(mesh):
    placed = (
        P("section", "expert", None),
        P("section", "expert"),
        P("section", "expert"),
        P("section", "expert"),
        P("section", None, None),
        P("section", None, None),
        P("section", None, "expert"),
        P("section", "expert", None),
    )
    return jax.shard_map(
        body, mesh=mesh, in_specs=placed, out_specs=P("section", "expert", None), check_vma=False
    )
```

```python
import jax
import jax.numpy as jnp
from jax import lax
from jax.experimental import pallas as pl
from jax.experimental.pallas import tpu as pltpu
from jax.sharding import PartitionSpec as P

HEAD_DIM = 64
CAP = 40
NX, NZ, NY = 4, 2, 4
CHUNKS = ((0, 1152, 2048), (2048, 3200, 4096))
PLACE = (0, 40, 120, 80)


def shift(value, dx=0, dz=0, dy=0):
    pairs = []
    for x in range(NX):
        for z in range(NZ):
            for y in range(NY):
                to = ((x + dx) % NX * NZ + (z + dz) % NZ) * NY + (y + dy) % NY
                pairs.append(((x * NZ + z) * NY + y, to))
    return lax.ppermute(value, "expert", pairs)


def dot32(a, b):
    return jnp.dot(a, b, preferred_element_type=jnp.float32)


def half(value):
    return value.astype(jnp.bfloat16)


def rms_scale(values, gain_row):
    mean_sq = jnp.mean(values * values, axis=-1, keepdims=True)
    return values * lax.rsqrt(mean_sq + 1e-06) * gain_row


def after(value, *earlier):
    return lax.optimization_barrier((value, *earlier))[0]


def rows(*blocks):
    return jnp.concatenate(blocks, axis=0)


def gather(p0, p1, p3, p2, w_first):
    def first(*blocks):
        h = half(jnp.maximum(dot32(rows(*blocks), w_first), 0.0))
        cuts, start = [], 0
        for block in blocks:
            cuts.append(h[start : start + block.shape[0]])
            start += block.shape[0]
        return cuts

    r2 = shift(p2, dx=2)
    r1 = shift(p1, dx=1)
    r3 = shift(p3, dx=-1)
    b0 = shift(p0, dy=1)
    a0 = shift(p0, dy=-1)
    o0 = shift(after(p0, b0, a0), dz=1)
    g1 = after(rows(r1, r3, r2), o0)
    b1 = shift(g1, dy=1)
    a1 = shift(g1, dy=-1)
    po = shift(g1[:88], dz=1)
    h_p0, h_b0, h_a0 = first(p0, b0, a0)
    near0 = shift(after(rows(b0, a0), po), dz=1)
    fb = shift(after(rows(b0[:16], b1[:64]), a1), dy=1)
    fa = shift(after(rows(a0[16:], a1[64:]), b1), dy=-1)
    h_g1, h_b1, h_a1 = first(after(g1, near0), b1, a1)
    zq = shift(after(rows(g1[88:], b1[88:], a1[88:]), near0), dz=1)
    pb = shift(after(po, near0), dy=1)
    pa = shift(after(po, near0), dy=-1)
    h_o0, h_near0 = first(o0, near0)
    h_fb, h_fa = first(fb, fa)
    zf = shift(after(rows(fb[:16], fa[:24], fa[48:]), zq), dz=1)
    pbh = shift(after(pb[:48], pa), dy=1)
    pah = shift(after(pa[48:], pb), dy=-1)
    h_po, h_pb, h_pa = first(po, pb, pa)
    (h_zq,) = first(zq)
    h_pbh, h_pah, h_zf = first(pbh, pah, zf)
    return {
        (0, 0): rows(h_p0, h_g1),
        (0, -1): rows(h_b0, h_b1),
        (0, 1): rows(h_a0, h_a1),
        (0, 2): rows(h_fb[:16], h_fa[:24], h_fb[16:], h_fa[24:]),
        (1, 0): rows(h_o0, h_po, h_zq[:32]),
        (1, -1): rows(h_near0[:40], h_pb, h_zq[32:64]),
        (1, 1): rows(h_near0[40:], h_pa, h_zq[64:]),
        (1, 2): rows(h_zf[:40], h_pbh, h_pah, h_zf[40:]),
    }


def reduce_chunks(hid, w_second, chunks):
    f32 = jnp.float32
    a = {k: v[:80] for k, v in hid.items()}
    b = {k: v[80:] for k, v in hid.items()}
    up1 = rows(a[1, 2], a[0, 2], b[1, 1], b[0, 1])
    down1 = rows(b[1, 2], b[0, 2], a[1, -1], a[0, -1])
    up2 = rows(a[1, 1], a[0, 1])
    down2 = rows(b[1, -1], b[0, -1])
    up3 = rows(a[0, 2], b[0, 1])
    down3 = rows(b[0, 2], a[0, -1])
    own_a = rows(a[1, 0], a[0, 0])
    own_b = rows(b[1, 0], b[0, 0])
    away = rows(hid[1, 2], hid[1, 1], hid[1, -1], hid[1, 0])
    (wy1, wz1), (wy2, wz2) = [(w_second[:, y], w_second[:, z]) for y, z in chunks]

    def part(h, w, *more):
        out = dot32(h, w)
        for m in more:
            out = out + m.astype(f32)
        return half(out)

    def start(w, *earlier):
        ru = shift(after(part(up1, w), *earlier), dy=1)
        rd = shift(after(part(down1, w), *earlier), dy=-1)
        return ru, rd

    def second(w, ru, rd, *earlier):
        su = shift(after(part(up2, w, ru[:160]), *earlier), dy=1)
        sd = shift(after(part(down2, w, rd[:160]), *earlier), dy=-1)
        return su, sd

    def sums(w, ru, rd, su, sd):
        sum_a = dot32(own_a, w) + rd[160:].astype(f32) + su.astype(f32)
        sum_b = dot32(own_b, w) + ru[160:].astype(f32) + sd.astype(f32)
        return half(rows(sum_a[:80], sum_b[:80])), rows(sum_a[80:], sum_b[80:])

    def third(w, g, *earlier):
        tu = shift(after(part(up3, w, rows(g[:80], g[240:320])), *earlier), dy=1)
        td = shift(after(part(down3, w, rows(g[80:160], g[320:400])), *earlier), dy=-1)
        return tu, td

    def fourth(w, g, tu, td):
        vu = shift(part(a[0, 1], w, g[160:240], tu[:80]), dy=1)
        vd = shift(part(b[0, -1], w, g[400:480], td[:80]), dy=-1)
        return vu, vd

    def total(w, g, kept, e, tu, td, vu, vd):
        z = rows(
            part(a[0, 0], w, g[480:560], td[80:], vu), part(b[0, 0], w, g[560:], tu[80:], vd)
        )
        return jnp.concatenate([half(kept + e.astype(f32)), z], axis=1)

    ru1, rd1 = start(wy1)
    g1 = shift(part(away, wz1), dz=1)
    su1, sd1 = second(wy1, ru1, rd1)
    ru2, rd2 = start(wy2, ru1, rd1)
    g2 = shift(after(part(away, wz2), g1), dz=1)
    tu1, td1 = third(wz1, g1, su1, sd1)
    su2, sd2 = second(wy2, ru2, rd2)
    sent1, kept1 = sums(wy1, ru1, rd1, su1, sd1)
    vu1, vd1 = fourth(wz1, g1, tu1, td1)
    e1 = shift(after(sent1, g2), dz=1)
    tu2, td2 = third(wz2, g2, su2, sd2)
    sent2, kept2 = sums(wy2, ru2, rd2, su2, sd2)
    e2 = shift(after(sent2, vu1, vd1, e1), dz=1)
    vu2, vd2 = fourth(wz2, g2, tu2, td2)
    total1 = total(wz1, g1, kept1, e1, tu1, td1, vu1, vd1)
    total2 = total(wz2, g2, kept2, e2, tu2, td2, vu2, vd2)
    return total1, total2


def full(memory_space=pltpu.VMEM):
    return pl.BlockSpec(memory_space=memory_space)


def dispatch_kernel(x_ref, acts_ref, gain_ref, chosen_ref, slot_ref, *outs):
    f32 = jnp.float32
    count, features = acts_ref.shape
    step = 512
    square = jnp.zeros((count, 128), f32)
    for c in range(0, features, step):
        v = acts_ref[:, c : c + step].astype(f32)
        v = v * v
        for k in range(0, step, 128):
            square = square + v[:, k : k + 128]
    scale = lax.rsqrt(jnp.sum(square, axis=1, keepdims=True) / features + 1e-06)
    ahead = (chosen_ref[...] - x_ref[0] + NX) & (NX - 1)
    slot = slot_ref[...]
    maps = []
    for d in (0, 1, 3, 2):
        place = jnp.where((slot >= 0) & (ahead == d), slot, -1)
        maps.append((lax.broadcasted_iota(jnp.int32, (CAP, count), 0) == place).astype(jnp.bfloat16))
    for c in range(0, features, step):
        cols = slice(c, c + step)
        normed = (acts_ref[:, cols].astype(f32) * scale * gain_ref[0:1, cols]).astype(jnp.bfloat16)
        for out, pick in zip(outs, maps):
            out[:, cols] = dot32(pick, normed).astype(jnp.bfloat16)


def dispatch(my_x, acts, gains, chosen, slots):
    features = acts.shape[1]
    block = jax.ShapeDtypeStruct((CAP, features), jnp.bfloat16)
    return pl.pallas_call(
        dispatch_kernel,
        out_shape=[block] * 4,
        in_specs=[full(pltpu.SMEM)] + [full()] * 4,
        out_specs=[full()] * 4,
        compiler_params=pltpu.CompilerParams(vmem_limit_bytes=24 << 20),
        cost_estimate=pl.CostEstimate(flops=4 * 160 * 128 * features, bytes_accessed=4 << 20, transcendentals=128),
    )(my_x.reshape(1), acts, gains, chosen, slots)


def attention_kernel(decoder_ref, lay1, lay2, n1, f1, b1, n2, f2, b2, gain_ref, out_ref, side, memory):
    f32 = jnp.float32
    count, first = lay1.shape
    features = out_ref.shape[1]
    decoder = decoder_ref[0]
    step = 256

    def lay_cols(c):
        return lay1[:, c : c + step] if c < first else lay2[:, c - first : c - first + step]

    def source_cols(c, part):
        refs, c = ((n1, f1, b1), c) if c < first else ((n2, f2, b2), c - first)
        near, far, beside = [ref[part, c : c + step].astype(f32) for ref in refs]
        return near + far + beside

    @pl.when(decoder == 0)
    def _():
        for c in range(0, features, step):
            out_ref[:, c : c + step] = lay_cols(c)

    @pl.when(decoder == 1)
    def _():
        squares = [jnp.zeros((count, 128), f32), jnp.zeros((count, 128), f32)]
        token_rows, extra_rows = slice(0, count), slice(count, count + 16)
        for c in range(0, features, step):
            source = source_cols(c, token_rows)
            memory[:, c : c + step] = source.astype(jnp.bfloat16)
            for i, v in enumerate((lay_cols(c).astype(f32), source)):
                v = v * v
                for k in range(0, step, 128):
                    squares[i] = squares[i] + v[:, k : k + 128]
        scales = [lax.rsqrt(jnp.sum(s, axis=1, keepdims=True) / features + 1e-06) for s in squares]
        for c in range(0, features, step):
            cols = slice(c, c + step)
            side[:, cols] = (lay_cols(c).astype(f32) * scales[0] * gain_ref[1:2, cols]).astype(jnp.bfloat16)
            extra = source_cols(c % first + first, extra_rows)[4 * (c // first) :]
            gain = extra[0:1] + extra[1:2] + extra[2:3]
            memory[:, cols] = (memory[:, cols].astype(f32) * scales[1] * gain).astype(jnp.bfloat16)
        length = source_cols(first, extra_rows)[3:4, :count]
        live = lax.broadcasted_iota(jnp.int32, (1, count), 1).astype(f32) < length
        head_of = lax.broadcasted_iota(jnp.int32, (1, step), 1) // HEAD_DIM
        heads = step // HEAD_DIM
        for c in range(0, features, step):
            cols = slice(c, c + step)
            query, keys = side[:, cols], memory[:, cols]
            zero = jnp.zeros_like(query)
            stacked = rows(*[jnp.where(head_of == h, query, zero) for h in range(heads)])
            scores = lax.dot_general(
                stacked, keys, (((1,), (1,)), ((), ())), preferred_element_type=f32
            )
            scores = jnp.where(live, scores * (HEAD_DIM**-0.5), f32(-1e30))
            expo = jnp.exp(scores - jnp.max(scores, axis=1, keepdims=True))
            weights = (expo / jnp.sum(expo, axis=1, keepdims=True)).astype(jnp.bfloat16)
            found = dot32(weights, keys)
            context = jnp.zeros((count, step), f32)
            for h in range(heads):
                context = jnp.where(head_of == h, found[h * count : (h + 1) * count], context)
            out_ref[:, cols] = (lay_cols(c).astype(f32) + context).astype(jnp.bfloat16)


def attention(decoder, lay1, lay2, n1, f1, b1, n2, f2, b2, gains):
    count, features = lay1.shape[0], gains.shape[1]
    whole = (count, features)
    return pl.pallas_call(
        attention_kernel,
        out_shape=jax.ShapeDtypeStruct(whole, jnp.bfloat16),
        in_specs=[full(pltpu.SMEM)] + [full()] * 9,
        out_specs=full(),
        scratch_shapes=[pltpu.VMEM(whole, jnp.bfloat16)] * 2,
        compiler_params=pltpu.CompilerParams(vmem_limit_bytes=32 << 20),
        cost_estimate=pl.CostEstimate(flops=1 << 30, bytes_accessed=8 << 20, transcendentals=1 << 20),
    )(decoder.reshape(1), lay1, lay2, n1, f1, b1, n2, f2, b2, gains)


def body(
    arriving_state,
    stream_extent,
    word_specialist_choice,
    capacity_places,
    rescale_factors,
    gating_columns,
    specialist_entry_matrix,
    specialist_exit_matrix,
):
    f32 = jnp.float32
    acts = arriving_state[0]
    row_count, features = acts.shape
    enc_count = lax.axis_size("section") // 2
    section_index = lax.axis_index("section")
    my_x = lax.axis_index("expert") // (NZ * NY)
    gain_rows = rescale_factors[0]
    route_cols = gating_columns[0]
    experts = route_cols.shape[1]
    w_first = specialist_entry_matrix[0]
    w_second = specialist_exit_matrix[0]

    acts_wide = acts.astype(f32)
    normed = rms_scale(acts_wide, gain_rows[0]).astype(jnp.bfloat16)
    chosen = word_specialist_choice[0]
    slot_ids = capacity_places[0]
    is_live = slot_ids >= 0
    ahead = (chosen - my_x + NX) % NX
    start = jnp.where(ahead == 2, PLACE[2], jnp.where(ahead == 3, PLACE[3], ahead * CAP))
    target = jnp.where(is_live, start + slot_ids, -1)
    places = jnp.arange(experts * CAP, dtype=jnp.int32)
    blocks = dispatch(my_x, acts, gain_rows, word_specialist_choice, capacity_places)

    hid = gather(*blocks, w_first)

    logits = jnp.dot(normed.astype(f32), route_cols, precision=lax.Precision.HIGHEST)
    picks = chosen[:, None] == jnp.arange(experts, dtype=jnp.int32)[None, :]
    gate_value = jax.nn.sigmoid(jnp.sum(jnp.where(picks, logits, 0.0), axis=1))
    gate = jnp.where(is_live, gate_value, 0.0)[:, None]
    combine_map = (target[:, None] == places[None, :]).astype(jnp.bfloat16)

    gain = gain_rows[1]
    high = half(gain)
    mid = half(gain - high.astype(f32))
    low = half(gain - high.astype(f32) - mid.astype(f32))
    extra = jnp.stack([high, mid, low, jnp.full((features,), stream_extent[0, 0].astype(jnp.bfloat16))])
    extra = rows(extra[:, : features // 2], extra[:, features // 2 :], jnp.zeros((8, features // 2), jnp.bfloat16))
    layer_cols, source_cols = [], []
    chunks = [(slice(a, b), slice(b, c)) for a, b, c in CHUNKS]
    last = enc_count - 1
    for (lo, _, hi), total in zip(CHUNKS, reduce_chunks(hid, w_second, chunks)):
        kept = total[:40]
        if layer_cols:
            total = after(total, layer_cols[0])
            kept = after(kept, source_cols[0], source_cols[1])
        back = rows(
            kept,
            shift(total[40:80], dx=-1),
            shift(total[80:120], dx=1),
            shift(total[120:160], dx=-2),
        )
        cols = half(acts_wide[:, lo:hi] + gate * dot32(combine_map, back))
        layer_cols.append(cols)
        message = cols if lo == 0 else rows(cols, extra)
        near = lax.ppermute(message, "section", [(last, last + 2)])
        far = lax.ppermute(message, "section", [(last, last + 4)])
        beside = lax.ppermute(near + far, "section", [(last + 2, last + 1), (last + 4, last + 3)])
        source_cols += [near, far, beside]
    decoder = (section_index >= enc_count).astype(jnp.int32)
    return attention(decoder, *layer_cols, *source_cols, gain_rows)[None]


def solution(mesh):
    placed = (
        P("section", "expert", None),
        P("section", "expert"),
        P("section", "expert"),
        P("section", "expert"),
        P("section", None, None),
        P("section", None, None),
        P("section", None, "expert"),
        P("section", "expert", None),
    )
    return jax.shard_map(
        body, mesh=mesh, in_specs=placed, out_specs=P("section", "expert", None), check_vma=False
    )
```

```python
import jax
import jax.numpy as jnp
from jax import lax
from jax.experimental import pallas as pl
from jax.experimental.pallas import tpu as pltpu
from jax.sharding import PartitionSpec as P

HEAD_DIM = 64
CAP = 40
NX, NZ, NY = 4, 2, 4
CHUNKS = ((0, 1152, 2048), (2048, 3200, 4096))
PLACE = (0, 40, 120, 80)


def shift(value, dx=0, dz=0, dy=0):
    pairs = []
    for x in range(NX):
        for z in range(NZ):
            for y in range(NY):
                to = ((x + dx) % NX * NZ + (z + dz) % NZ) * NY + (y + dy) % NY
                pairs.append(((x * NZ + z) * NY + y, to))
    return lax.ppermute(value, "expert", pairs)


def dot32(a, b):
    return jnp.dot(a, b, preferred_element_type=jnp.float32)


def half(value):
    return value.astype(jnp.bfloat16)


def rms_scale(values, gain_row):
    mean_sq = jnp.mean(values * values, axis=-1, keepdims=True)
    return values * lax.rsqrt(mean_sq + 1e-06) * gain_row


def after(value, *earlier):
    return lax.optimization_barrier((value, *earlier))[0]


def rows(*blocks):
    return jnp.concatenate(blocks, axis=0)


def gather(p0, p1, p3, p2, w_first):
    def first(*blocks):
        h = half(jnp.maximum(dot32(rows(*blocks), w_first), 0.0))
        cuts, start = [], 0
        for block in blocks:
            cuts.append(h[start : start + block.shape[0]])
            start += block.shape[0]
        return cuts

    r2 = shift(p2, dx=2)
    r1 = shift(p1, dx=1)
    r3 = shift(p3, dx=-1)
    b0 = shift(p0, dy=1)
    a0 = shift(p0, dy=-1)
    o0 = shift(after(p0, b0, a0), dz=1)
    g1 = after(rows(r1, r3, r2), o0)
    b1 = shift(g1, dy=1)
    a1 = shift(g1, dy=-1)
    po = shift(g1[:88], dz=1)
    h_p0, h_b0, h_a0 = first(p0, b0, a0)
    near0 = shift(after(rows(b0, a0), po), dz=1)
    fb = shift(after(rows(b0[:16], b1[:64]), a1), dy=1)
    fa = shift(after(rows(a0[16:], a1[64:]), b1), dy=-1)
    h_g1, h_b1, h_a1 = first(after(g1, near0), b1, a1)
    zq = shift(after(rows(g1[88:], b1[88:], a1[88:]), near0), dz=1)
    pb = shift(after(po, near0), dy=1)
    pa = shift(after(po, near0), dy=-1)
    h_o0, h_near0 = first(o0, near0)
    h_fb, h_fa = first(fb, fa)
    zf = shift(after(rows(fb[:16], fa[:24], fa[48:]), zq), dz=1)
    pbh = shift(after(pb[:48], pa), dy=1)
    pah = shift(after(pa[48:], pb), dy=-1)
    h_po, h_pb, h_pa = first(po, pb, pa)
    (h_zq,) = first(zq)
    h_pbh, h_pah, h_zf = first(pbh, pah, zf)
    return {
        (0, 0): rows(h_p0, h_g1),
        (0, -1): rows(h_b0, h_b1),
        (0, 1): rows(h_a0, h_a1),
        (0, 2): rows(h_fb[:16], h_fa[:24], h_fb[16:], h_fa[24:]),
        (1, 0): rows(h_o0, h_po, h_zq[:32]),
        (1, -1): rows(h_near0[:40], h_pb, h_zq[32:64]),
        (1, 1): rows(h_near0[40:], h_pa, h_zq[64:]),
        (1, 2): rows(h_zf[:40], h_pbh, h_pah, h_zf[40:]),
    }


def reduce_chunks(hid, w_second, chunks):
    f32 = jnp.float32
    a = {k: v[:80] for k, v in hid.items()}
    b = {k: v[80:] for k, v in hid.items()}
    up1 = rows(a[1, 2], a[0, 2], b[1, 1], b[0, 1])
    down1 = rows(b[1, 2], b[0, 2], a[1, -1], a[0, -1])
    up2 = rows(a[1, 1], a[0, 1])
    down2 = rows(b[1, -1], b[0, -1])
    up3 = rows(a[0, 2], b[0, 1])
    down3 = rows(b[0, 2], a[0, -1])
    own_a = rows(a[1, 0], a[0, 0])
    own_b = rows(b[1, 0], b[0, 0])
    away = rows(hid[1, 2], hid[1, 1], hid[1, -1], hid[1, 0])
    (wy1, wz1), (wy2, wz2) = [(w_second[:, y], w_second[:, z]) for y, z in chunks]

    def part(h, w, *more):
        out = dot32(h, w)
        for m in more:
            out = out + m.astype(f32)
        return half(out)

    def start(w, *earlier):
        ru = shift(after(part(up1, w), *earlier), dy=1)
        rd = shift(after(part(down1, w), *earlier), dy=-1)
        return ru, rd

    def second(w, ru, rd, *earlier):
        su = shift(after(part(up2, w, ru[:160]), *earlier), dy=1)
        sd = shift(after(part(down2, w, rd[:160]), *earlier), dy=-1)
        return su, sd

    def sums(w, ru, rd, su, sd):
        sum_a = dot32(own_a, w) + rd[160:].astype(f32) + su.astype(f32)
        sum_b = dot32(own_b, w) + ru[160:].astype(f32) + sd.astype(f32)
        return half(rows(sum_a[:80], sum_b[:80])), rows(sum_a[80:], sum_b[80:])

    def third(w, g, *earlier):
        tu = shift(after(part(up3, w, rows(g[:80], g[240:320])), *earlier), dy=1)
        td = shift(after(part(down3, w, rows(g[80:160], g[320:400])), *earlier), dy=-1)
        return tu, td

    def fourth(w, g, tu, td):
        vu = shift(part(a[0, 1], w, g[160:240], tu[:80]), dy=1)
        vd = shift(part(b[0, -1], w, g[400:480], td[:80]), dy=-1)
        return vu, vd

    def total(w, g, kept, e, tu, td, vu, vd):
        z = rows(
            part(a[0, 0], w, g[480:560], td[80:], vu), part(b[0, 0], w, g[560:], tu[80:], vd)
        )
        return jnp.concatenate([half(kept + e.astype(f32)), z], axis=1)

    ru1, rd1 = start(wy1)
    g1 = shift(part(away, wz1), dz=1)
    su1, sd1 = second(wy1, ru1, rd1)
    ru2, rd2 = start(wy2, ru1, rd1)
    g2 = shift(after(part(away, wz2), g1), dz=1)
    tu1, td1 = third(wz1, g1, su1, sd1)
    su2, sd2 = second(wy2, ru2, rd2)
    sent1, kept1 = sums(wy1, ru1, rd1, su1, sd1)
    vu1, vd1 = fourth(wz1, g1, tu1, td1)
    e1 = shift(after(sent1, g2), dz=1)
    tu2, td2 = third(wz2, g2, su2, sd2)
    sent2, kept2 = sums(wy2, ru2, rd2, su2, sd2)
    e2 = shift(after(sent2, vu1, vd1, e1), dz=1)
    vu2, vd2 = fourth(wz2, g2, tu2, td2)
    total1 = total(wz1, g1, kept1, e1, tu1, td1, vu1, vd1)
    total2 = total(wz2, g2, kept2, e2, tu2, td2, vu2, vd2)
    return total1, total2


def full(memory_space=pltpu.VMEM):
    return pl.BlockSpec(memory_space=memory_space)


def dispatch_kernel(x_ref, acts_ref, gain_ref, chosen_ref, slot_ref, *outs):
    f32 = jnp.float32
    count, features = acts_ref.shape
    step = 512
    square = jnp.zeros((count, 128), f32)
    for c in range(0, features, step):
        v = acts_ref[:, c : c + step].astype(f32)
        v = v * v
        for k in range(0, step, 128):
            square = square + v[:, k : k + 128]
    scale = lax.rsqrt(jnp.sum(square, axis=1, keepdims=True) / features + 1e-06)
    ahead = (chosen_ref[...] - x_ref[0] + NX) & (NX - 1)
    slot = slot_ref[...]
    maps = []
    for d in (0, 1, 3, 2):
        place = jnp.where((slot >= 0) & (ahead == d), slot, -1)
        maps.append((lax.broadcasted_iota(jnp.int32, (CAP, count), 0) == place).astype(jnp.bfloat16))
    for c in range(0, features, step):
        cols = slice(c, c + step)
        normed = (acts_ref[:, cols].astype(f32) * scale * gain_ref[0:1, cols]).astype(jnp.bfloat16)
        for out, pick in zip(outs, maps):
            out[:, cols] = dot32(pick, normed).astype(jnp.bfloat16)


def dispatch(my_x, acts, gains, chosen, slots):
    features = acts.shape[1]
    block = jax.ShapeDtypeStruct((CAP, features), jnp.bfloat16)
    return pl.pallas_call(
        dispatch_kernel,
        out_shape=[block] * 4,
        in_specs=[full(pltpu.SMEM)] + [full()] * 4,
        out_specs=[full()] * 4,
        compiler_params=pltpu.CompilerParams(vmem_limit_bytes=24 << 20),
        cost_estimate=pl.CostEstimate(flops=4 * 160 * 128 * features, bytes_accessed=4 << 20, transcendentals=128),
    )(my_x.reshape(1), acts, gains, chosen, slots)


def attention_kernel(decoder_ref, lay1, lay2, n1, f1, b1, n2, f2, b2, gain_ref, out_ref, side, memory):
    f32 = jnp.float32
    count, first = lay1.shape
    features = out_ref.shape[1]
    decoder = decoder_ref[0]
    step = 256

    def lay_cols(c):
        return lay1[:, c : c + step] if c < first else lay2[:, c - first : c - first + step]

    def source_cols(c, part):
        refs, c = ((n1, f1, b1), c) if c < first else ((n2, f2, b2), c - first)
        near, far, beside = [ref[part, c : c + step].astype(f32) for ref in refs]
        return near + far + beside

    @pl.when(decoder == 0)
    def _():
        for c in range(0, features, step):
            out_ref[:, c : c + step] = lay_cols(c)

    @pl.when(decoder == 1)
    def _():
        squares = [jnp.zeros((count, 128), f32), jnp.zeros((count, 128), f32)]
        token_rows, extra_rows = slice(0, count), slice(count, count + 16)
        for c in range(0, features, step):
            source = source_cols(c, token_rows)
            memory[:, c : c + step] = source.astype(jnp.bfloat16)
            for i, v in enumerate((lay_cols(c).astype(f32), source)):
                v = v * v
                for k in range(0, step, 128):
                    squares[i] = squares[i] + v[:, k : k + 128]
        scales = [lax.rsqrt(jnp.sum(s, axis=1, keepdims=True) / features + 1e-06) for s in squares]
        for c in range(0, features, step):
            cols = slice(c, c + step)
            side[:, cols] = (lay_cols(c).astype(f32) * scales[0] * gain_ref[1:2, cols]).astype(jnp.bfloat16)
            extra = source_cols(c % first + first, extra_rows)[4 * (c // first) :]
            gain = extra[0:1] + extra[1:2] + extra[2:3]
            memory[:, cols] = (memory[:, cols].astype(f32) * scales[1] * gain).astype(jnp.bfloat16)
        length = source_cols(first, extra_rows)[3:4, :count]
        live = lax.broadcasted_iota(jnp.int32, (count, 1), 0).astype(f32) < length[:, :1]
        head_of = lax.broadcasted_iota(jnp.int32, (1, step), 1) // HEAD_DIM
        heads = step // HEAD_DIM
        for c in range(0, features, step):
            cols = slice(c, c + step)
            query, keys = side[:, cols], memory[:, cols]
            zero = jnp.zeros_like(query)
            stacked = rows(*[jnp.where(head_of == h, query, zero) for h in range(heads)])
            scores = lax.dot_general(
                keys, stacked, (((1,), (1,)), ((), ())), preferred_element_type=f32
            )
            scores = jnp.where(live, scores * (HEAD_DIM**-0.5), f32(-1e30))
            expo = jnp.exp(scores - jnp.max(scores, axis=0, keepdims=True))
            weights = (expo * (1.0 / jnp.sum(expo, axis=0, keepdims=True))).astype(jnp.bfloat16)
            found = lax.dot_general(
                weights, keys, (((0,), (0,)), ((), ())), preferred_element_type=f32
            )
            context = jnp.zeros((count, step), f32)
            for h in range(heads):
                context = jnp.where(head_of == h, found[h * count : (h + 1) * count], context)
            out_ref[:, cols] = (lay_cols(c).astype(f32) + context).astype(jnp.bfloat16)


def attention(decoder, lay1, lay2, n1, f1, b1, n2, f2, b2, gains):
    count, features = lay1.shape[0], gains.shape[1]
    whole = (count, features)
    return pl.pallas_call(
        attention_kernel,
        out_shape=jax.ShapeDtypeStruct(whole, jnp.bfloat16),
        in_specs=[full(pltpu.SMEM)] + [full()] * 9,
        out_specs=full(),
        scratch_shapes=[pltpu.VMEM(whole, jnp.bfloat16)] * 2,
        compiler_params=pltpu.CompilerParams(vmem_limit_bytes=32 << 20),
        cost_estimate=pl.CostEstimate(flops=1 << 30, bytes_accessed=8 << 20, transcendentals=1 << 20),
    )(decoder.reshape(1), lay1, lay2, n1, f1, b1, n2, f2, b2, gains)


def body(
    arriving_state,
    stream_extent,
    word_specialist_choice,
    capacity_places,
    rescale_factors,
    gating_columns,
    specialist_entry_matrix,
    specialist_exit_matrix,
):
    f32 = jnp.float32
    acts = arriving_state[0]
    row_count, features = acts.shape
    enc_count = lax.axis_size("section") // 2
    section_index = lax.axis_index("section")
    my_x = lax.axis_index("expert") // (NZ * NY)
    gain_rows = rescale_factors[0]
    route_cols = gating_columns[0]
    experts = route_cols.shape[1]
    w_first = specialist_entry_matrix[0]
    w_second = specialist_exit_matrix[0]

    acts_wide = acts.astype(f32)
    normed = rms_scale(acts_wide, gain_rows[0]).astype(jnp.bfloat16)
    chosen = word_specialist_choice[0]
    slot_ids = capacity_places[0]
    is_live = slot_ids >= 0
    ahead = (chosen - my_x + NX) % NX
    start = jnp.where(ahead == 2, PLACE[2], jnp.where(ahead == 3, PLACE[3], ahead * CAP))
    target = jnp.where(is_live, start + slot_ids, -1)
    places = jnp.arange(experts * CAP, dtype=jnp.int32)
    blocks = dispatch(my_x, acts, gain_rows, word_specialist_choice, capacity_places)

    hid = gather(*blocks, w_first)

    logits = jnp.dot(normed.astype(f32), route_cols, precision=lax.Precision.HIGHEST)
    picks = chosen[:, None] == jnp.arange(experts, dtype=jnp.int32)[None, :]
    gate_value = jax.nn.sigmoid(jnp.sum(jnp.where(picks, logits, 0.0), axis=1))
    gate = jnp.where(is_live, gate_value, 0.0)[:, None]
    combine_map = (target[:, None] == places[None, :]).astype(jnp.bfloat16)

    gain = gain_rows[1]
    high = half(gain)
    mid = half(gain - high.astype(f32))
    low = half(gain - high.astype(f32) - mid.astype(f32))
    extra = jnp.stack([high, mid, low, jnp.full((features,), stream_extent[0, 0].astype(jnp.bfloat16))])
    extra = rows(extra[:, : features // 2], extra[:, features // 2 :], jnp.zeros((8, features // 2), jnp.bfloat16))
    layer_cols, source_cols = [], []
    chunks = [(slice(a, b), slice(b, c)) for a, b, c in CHUNKS]
    last = enc_count - 1
    for (lo, _, hi), total in zip(CHUNKS, reduce_chunks(hid, w_second, chunks)):
        kept = total[:40]
        if layer_cols:
            total = after(total, layer_cols[0])
            kept = after(kept, source_cols[0], source_cols[1])
        back = rows(
            kept,
            shift(total[40:80], dx=-1),
            shift(total[80:120], dx=1),
            shift(total[120:160], dx=-2),
        )
        cols = half(acts_wide[:, lo:hi] + gate * dot32(combine_map, back))
        layer_cols.append(cols)
        message = cols if lo == 0 else rows(cols, extra)
        near = lax.ppermute(message, "section", [(last, last + 2)])
        far = lax.ppermute(message, "section", [(last, last + 4)])
        beside = lax.ppermute(near + far, "section", [(last + 2, last + 1), (last + 4, last + 3)])
        source_cols += [near, far, beside]
    decoder = (section_index >= enc_count).astype(jnp.int32)
    return attention(decoder, *layer_cols, *source_cols, gain_rows)[None]


def solution(mesh):
    placed = (
        P("section", "expert", None),
        P("section", "expert"),
        P("section", "expert"),
        P("section", "expert"),
        P("section", None, None),
        P("section", None, None),
        P("section", None, "expert"),
        P("section", "expert", None),
    )
    return jax.shard_map(
        body, mesh=mesh, in_specs=placed, out_specs=P("section", "expert", None), check_vma=False
    )
```
